256 devices in a mesh: group: 16 (over y_hi, z), vocab: 16 (over y_lo, x, core).
Axes of the slice: x: 4, y: 4 (y_hi: 2, y_lo: 2; y = y_hi * 2 + y_lo), z: 8, core: 2. Of those that a mesh axis runs over, the one named last changes fastest.
Arguments:
- teacher_codes: bfloat16 [4096, 8192], P('vocab', 'group'), may hold values from -8 to 8
- block_scales: float32 [64, 4096], P('group', 'vocab'), may hold values from 0.3 to 3
- teacher_head: bfloat16 [8192, 16384], P('group', 'vocab'), may hold values from -0.25 to 0.25
- student_hidden: bfloat16 [4096, 2048], P('group', 'vocab'), may hold values from -12 to 12
- student_head: bfloat16 [2048, 16384], P(None, 'vocab'), may hold values from -0.5 to 0.5
- token_ids: int32 [4096], P('group'), may hold values from 0 to 16383
- loss_mask: int32 [4096], P('group'), may hold values from 0 to 1, as said below
Outputs:
- grad_hidden: bfloat16 [4096, 2048], P('group', 'vocab')
- token_loss: float32 [4096], P('group')
The draws below stay inside these ranges and needn't reach their ends.
Inputs may be any that keep to these rules, and one draw needn't show every extreme that they name: `loss_mask`: most tokens are live with a chance that rises from about 0.3 at the first token to about 0.9 at the last.
All inputs are finite; a program needn't handle non-finite values.
Results may differ from the reference program's by a relative error of at most 0.006.
Values may be sent and summed in bfloat16 or wider, within the bound.
No kernel may reach another device: no remote copies, remote signals or barrier semaphores. Data moves between devices by JAX's collectives and lax.ppermute only.
A program may use at most 128 MiB of HBM per device.

```python
import math
import jax
import jax.numpy as jnp
import numpy as np
from jax import lax

DT = 8192
DS = 2048
V = 16384
BLOCK = 128
TOKENS = 4096
NBLOCK = 64


def shared_pair(key, length, count):
    keys = jax.random.split(key, 2)
    signs = jnp.where(jax.random.uniform(keys[0], (length,), jnp.float32) < 0.5, -1.0, 1.0)
    picks = jax.random.randint(keys[1], (2,), 0, count)
    second = (picks[0] + 1 + picks[1] % (count - 1)) % count
    return (signs, picks[0], second)


def base_values(key, count, length):
    return jax.random.normal(key, (count, length), jnp.float32)


def head_draw(key, length, count, scale, reach, limit, family):
    signs, first, second = shared_pair(jax.random.fold_in(key, family), length, count)
    key = jax.random.fold_in(key, family + 1)
    values = base_values(key, length, count) * scale
    column = signs * (reach / length)
    columns = jnp.arange(count, dtype=jnp.int32)[None, :]
    values = jnp.where(columns == first, column[:, None], values)
    values = jnp.where(columns == second, (0.993 * column)[:, None], values)
    return jnp.clip(values, -limit, limit)


def rows_draw(key, count, length, family, offset, least, spread, limit):
    signs, first, second = shared_pair(jax.random.fold_in(key, family), length, V)
    key = jax.random.fold_in(key, family + 2)
    values = base_values(key, count, length)
    rows = jnp.arange(count, dtype=jnp.int32)
    strength = least + spread * (rows * 5 % 7).astype(jnp.float32) / 6.0
    aligned = rows % 61 == offset
    values = jnp.where(aligned[:, None], strength[:, None] * signs[None, :], values)
    return jnp.clip(values, -limit, limit)


def draw_teacher_head(key, part):
    return head_draw(key, DT, V, 2.5 / math.sqrt(DT), 45.0, 0.25, 101).astype(jnp.bfloat16)


def draw_teacher_codes(key, part):
    return rows_draw(key, TOKENS, DT, 101, 7, 2.5, 5.0, 8.0).astype(jnp.bfloat16)


def draw_student_head(key, part):
    return head_draw(key, DS, V, 3.0 / math.sqrt(DS), 32.0, 0.5, 202).astype(jnp.bfloat16)


def draw_student_hidden(key, part):
    return rows_draw(key, TOKENS, DS, 202, 31, 4.5, 7.5, 12.0).astype(jnp.bfloat16)


def draw_loss_mask(key, part):
    key = jax.random.fold_in(key, 5)
    rows = jnp.arange(TOKENS, dtype=jnp.int32)
    ticket = jax.random.randint(key, (TOKENS,), 0, 600)
    forced = (rows % 61 == 7) | (rows % 61 == 31)
    return ((ticket < 180 + 360 * rows // TOKENS) | forced).astype(jnp.int32)


def touch_ends(drawn, rng, low, largest):
    longest = drawn.shape.index(max(drawn.shape))
    spots = []
    for shift in (0, 1):
        where = [jax.random.randint(jax.random.fold_in(rng, axis), (), 0, length) for axis, length in enumerate(drawn.shape)]
        where[longest] = (where[longest] + shift) % drawn.shape[longest]
        spots.append(tuple(where))
    return drawn.at[spots[0]].set(low).at[spots[1]].set(largest)


def block_scale(own_key, shape, cuts, smallest, high):
    def one(position, blocks):
        steps = jax.random.uniform(jax.random.fold_in(jax.random.fold_in(own_key, 6), position), (blocks,), jnp.float32, smallest / len(cuts), high / len(cuts))
        return jnp.repeat(jnp.exp(steps), shape[position] // blocks).reshape((-1,) + (1,) * (len(shape) - position - 1))

    gain = one(*cuts[0])
    for cut in cuts[1:]:
        gain = gain * one(*cut)
    return gain


def rank_bounds(count, slope):
    weights = [(1 << 20) // math.isqrt(rank ** slope) + 1 for rank in range(1, count + 1)]
    deviation = 1 + sum(weights) // (1 << 30)
    return np.cumsum(np.array([max(1, weight // deviation) for weight in weights]))


def skewed_ids(own_key, extent, number_of, lean):
    table = rank_bounds(number_of, lean)
    ticket = jax.random.randint(jax.random.fold_in(own_key, 1), extent, 0, int(table[number_of - 1]))
    rank = jnp.searchsorted(jnp.asarray(table, jnp.int32), ticket, side="right")
    return jax.random.permutation(jax.random.fold_in(own_key, 2), number_of)[rank].astype(jnp.int32)


def setup_inputs(seed: int = 0) -> dict:
    arg_keys = jax.random.split(jax.random.key(seed), 8)
    teacher_codes = draw_teacher_codes(jax.random.fold_in(arg_keys[7], 71), 0)
    block_scales = jnp.clip(jnp.exp(math.log(3.0) - 2.3025851 * jax.random.uniform(arg_keys[1], (NBLOCK, TOKENS), jnp.float32) ** block_scale(arg_keys[1], (NBLOCK, TOKENS), ((0, 16), (1, 16)), -0.2, 0.2)), 0.3, 3.0)
    teacher_head = draw_teacher_head(jax.random.fold_in(arg_keys[7], 71), 0)
    student_hidden = draw_student_hidden(jax.random.fold_in(arg_keys[7], 71), 0)
    student_head = draw_student_head(jax.random.fold_in(arg_keys[7], 71), 0)
    token_ids = touch_ends(skewed_ids(arg_keys[5], (TOKENS,), V, 2), jax.random.fold_in(arg_keys[5], 3), 0, V - 1).astype(jnp.int32)
    loss_mask = draw_loss_mask(jax.random.fold_in(arg_keys[7], 71), 0)
    return {"teacher_codes": teacher_codes, "block_scales": block_scales, "teacher_head": teacher_head, "student_hidden": student_hidden, "student_head": student_head, "token_ids": token_ids, "loss_mask": loss_mask}


CROSS_WEIGHT = 0.5


def dequantize(codes, scales):
    rows, cols = codes.shape
    blocks = codes.astype(jnp.float32).reshape(rows, cols // BLOCK, BLOCK) * jnp.transpose(scales)[:, :, None]
    return blocks.reshape(rows, cols).astype(jnp.bfloat16)


def reference(teacher_codes, block_scales, teacher_head, student_hidden, student_head, token_ids, loss_mask):
    teacher_rows = dequantize(teacher_codes, block_scales)
    teacher_logits = jnp.dot(teacher_rows, teacher_head, preferred_element_type=jnp.float32)
    student_logits = jnp.dot(student_hidden, student_head, preferred_element_type=jnp.float32)
    top_teacher = jnp.max(teacher_logits, axis=1)
    top_student = jnp.max(student_logits, axis=1)
    teacher_exp = jnp.exp(teacher_logits - top_teacher[:, None])
    student_exp = jnp.exp(student_logits - top_student[:, None])
    sum_teacher = jnp.sum(teacher_exp, axis=1)
    sum_student = jnp.sum(student_exp, axis=1)
    weighted = jnp.sum(teacher_exp * (teacher_logits - student_logits), axis=1)
    chosen = token_ids[:, None] == jnp.arange(V, dtype=jnp.int32)[None, :]
    target = jnp.sum(jnp.where(chosen, student_logits, 0.0), axis=1)
    divergence = weighted / sum_teacher - top_teacher - jnp.log(sum_teacher) + top_student + jnp.log(sum_student)
    cross_rows = top_student + jnp.log(sum_student) - target
    live_mask = loss_mask.astype(jnp.float32)
    token_loss = live_mask * (divergence + CROSS_WEIGHT * cross_rows)
    teacher_prob = teacher_exp / sum_teacher[:, None]
    student_prob = student_exp / sum_student[:, None]
    logit_grad = (live_mask[:, None] * ((1.0 + CROSS_WEIGHT) * student_prob - teacher_prob - CROSS_WEIGHT * chosen.astype(jnp.float32))).astype(jnp.bfloat16)
    grad_hidden = lax.dot_general(logit_grad, student_head, (((1,), (1,)), ((), ())), preferred_element_type=jnp.float32)
    return grad_hidden.astype(jnp.bfloat16), token_loss
```

```python
import jax
import jax.numpy as jnp
from jax import lax
from jax.experimental import pallas as pl
from jax.experimental.pallas import tpu as pltpu
from jax.sharding import Mesh
from jax.sharding import PartitionSpec as P

BLOCK = 128
CROSS_WEIGHT = 0.5
GROUP = ("yh", "z")
VOCAB = ("yl", "x", "c")
NZ = 8
CHUNKS = 4


def dequantize(codes, scales):
    rows, cols = codes.shape
    blocks = (
        codes.astype(jnp.float32).reshape(rows, cols // BLOCK, BLOCK)
        * jnp.transpose(scales)[:, :, None]
    )
    return blocks.reshape(rows, cols).astype(jnp.bfloat16)


def shift(x, s):
    return lax.ppermute(x, "z", [(i, (i + s) % NZ) for i in range(NZ)])


def after(x, gate):
    return lax.optimization_barrier((x, gate))[0]


def swap_rows_features():
    pairs = []
    for z in range(NZ):
        for x in range(4):
            for c in range(2):
                pairs.append(((z * 4 + x) * 2 + c, ((2 * x + c) * 4 + z // 2) * 2 + z % 2))
    return pairs


def chunk_kernel(where, rows, *refs):
    heads, (away, keep) = refs[:NZ], refs[NZ:]
    for side, out in ((0, away), (1, keep)):
        total = None
        for s in range(NZ):
            part = jnp.dot(rows[where[side, s]], heads[s][...], preferred_element_type=jnp.float32)
            total = part if total is None else total + part
        out[...] = total


def chunk_logits(where, rows, heads):
    tokens, width = rows.shape[1], heads[0].shape[1]
    out = jax.ShapeDtypeStruct((tokens, width), jnp.float32)
    vmem = pl.BlockSpec(memory_space=pltpu.VMEM)
    return pl.pallas_call(
        chunk_kernel,
        out_shape=(out, out),
        in_specs=[pl.BlockSpec(memory_space=pltpu.SMEM)] + [vmem] * (1 + NZ),
        out_specs=(vmem, vmem),
        compiler_params=pltpu.CompilerParams(vmem_limit_bytes=24 * 2**20),
        cost_estimate=pl.CostEstimate(
            flops=4 * tokens * width * NZ * rows.shape[2],
            bytes_accessed=rows.size * 2 + NZ * heads[0].size * 2 + 8 * tokens * width,
            transcendentals=0,
        ),
    )(where, rows, *heads)


def ring_chunks(head):
    width = head.shape[1] // CHUNKS
    results, gate = [], None
    for k in range(CHUNKS):
        own = head[:, k * width : (k + 1) * width]
        plus, minus = [own], [own]
        next_gate = None
        for s in range(1, 5):
            if s == 2 and gate is not None:
                plus[-1] = after(plus[-1], gate[0])
                minus[-1] = after(minus[-1], gate[1])
            if s < 4 or k % 2 == 0:
                plus.append(shift(plus[-1], 1))
            if s < 4 or k % 2 == 1:
                minus.append(shift(minus[-1], -1))
            if s == 2:
                next_gate = (plus[-1], minus[-1])
        gate = next_gate
        last = plus[4] if k % 2 == 0 else minus[4]
        results.append([own, plus[1], minus[1], plus[2], minus[2], plus[3], minus[3], last])
    return results


ORDER = (0, -1, 1, -2, 2, -3, 3, 4)


def body(
    teacher_codes, block_scales, teacher_head, student_hidden, student_head, token_ids, loss_mask
):
    yh, z = lax.axis_index("yh"), lax.axis_index("z")
    local_rows = dequantize(teacher_codes, block_scales)
    moved = lax.ppermute(local_rows, ("z", "x", "c"), swap_rows_features())
    rows = lax.all_gather(moved, VOCAB, axis=0, tiled=False)

    own_rows, features = student_hidden.shape
    hidden = lax.all_to_all(
        jnp.broadcast_to(student_hidden[None], (16,) + student_hidden.shape),
        VOCAB,
        split_axis=0,
        concat_axis=0,
        tiled=True,
    )
    hidden = jnp.transpose(hidden, (1, 0, 2)).reshape(own_rows, 16 * features)
    student_logits = jnp.dot(hidden, student_head, preferred_element_type=jnp.float32)
    shard_width = student_head.shape[1]
    columns = lax.axis_index(VOCAB) * shard_width + lax.broadcasted_iota(
        jnp.int32, (own_rows, shard_width), 1
    )
    chosen = token_ids[:, None] == columns
    target_part = jnp.sum(jnp.where(chosen, student_logits, 0.0), axis=1)

    slabs = lax.rem(z + jnp.array(ORDER, jnp.int32) + NZ, NZ)
    where = jnp.stack([(1 - yh) * NZ + slabs, yh * NZ + slabs])
    parts = []
    for heads in ring_chunks(teacher_head):
        away, keep = chunk_logits(where, rows, heads)
        parts.append(keep + lax.ppermute(away, "yh", [(0, 1), (1, 0)]))
    teacher_logits = jnp.concatenate(parts, axis=1)

    near_teacher = jnp.max(teacher_logits, axis=1)
    near_student = jnp.max(student_logits, axis=1)
    teacher_exp = jnp.exp(teacher_logits - near_teacher[:, None])
    student_exp = jnp.exp(student_logits - near_student[:, None])
    stats = jnp.stack(
        [
            near_teacher,
            jnp.sum(teacher_exp, axis=1),
            jnp.sum(teacher_exp * (teacher_logits - student_logits), axis=1),
            near_student,
            jnp.sum(student_exp, axis=1),
            target_part,
            jnp.zeros_like(target_part),
            jnp.zeros_like(target_part),
        ]
    )
    stats = lax.all_to_all(
        jnp.broadcast_to(stats[None], (16,) + stats.shape),
        VOCAB,
        split_axis=0,
        concat_axis=0,
        tiled=True,
    )
    top_teacher = jnp.max(stats[:, 0], axis=0)
    top_student = jnp.max(stats[:, 3], axis=0)
    scale_teacher = jnp.exp(stats[:, 0] - top_teacher[None])
    scale_student = jnp.exp(stats[:, 3] - top_student[None])
    sum_teacher = jnp.sum(stats[:, 1] * scale_teacher, axis=0)
    weighted = jnp.sum(stats[:, 2] * scale_teacher, axis=0)
    sum_student = jnp.sum(stats[:, 4] * scale_student, axis=0)
    target = jnp.sum(stats[:, 5], axis=0)

    divergence = (
        weighted / sum_teacher
        - top_teacher
        - jnp.log(sum_teacher)
        + top_student
        + jnp.log(sum_student)
    )
    cross_rows = top_student + jnp.log(sum_student) - target
    live_mask = loss_mask.astype(jnp.float32)
    token_loss = live_mask * (divergence + CROSS_WEIGHT * cross_rows)
    teacher_prob = jnp.exp(teacher_logits - top_teacher[:, None]) / sum_teacher[:, None]
    student_prob = jnp.exp(student_logits - top_student[:, None]) / sum_student[:, None]
    logit_grad = (
        live_mask[:, None]
        * (
            (1.0 + CROSS_WEIGHT) * student_prob
            - teacher_prob
            - CROSS_WEIGHT * chosen.astype(jnp.float32)
        )
    ).astype(jnp.bfloat16)
    hidden_terms = lax.dot_general(
        logit_grad, student_head, (((1,), (1,)), ((), ())), preferred_element_type=jnp.float32
    ).astype(jnp.bfloat16)
    hidden_terms = jnp.transpose(hidden_terms.reshape(own_rows, 16, features), (1, 0, 2))
    hidden_terms = lax.all_to_all(hidden_terms, VOCAB, split_axis=0, concat_axis=0, tiled=True)
    grad_hidden = jnp.sum(hidden_terms.astype(jnp.float32), axis=0).astype(jnp.bfloat16)
    return (grad_hidden, token_loss)


def solution(mesh):
    fine = Mesh(mesh.devices.reshape(2, NZ, 2, 4, 2), GROUP + VOCAB)
    placed = (
        P(VOCAB, GROUP),
        P(GROUP, VOCAB),
        P(GROUP, VOCAB),
        P(GROUP, VOCAB),
        P(None, VOCAB),
        P(GROUP),
        P(GROUP),
    )
    return jax.shard_map(
        body,
        mesh=fine,
        in_specs=placed,
        out_specs=(P(GROUP, VOCAB), P(GROUP)),
        check_vma=False,
    )
```

```python
import functools

import jax
import jax.numpy as jnp
from jax import lax
from jax.experimental import pallas as pl
from jax.experimental.pallas import tpu as pltpu
from jax.sharding import Mesh
from jax.sharding import PartitionSpec as P

BLOCK = 128
CROSS_WEIGHT = 0.5
GROUP = ("yh", "z")
VOCAB = ("yl", "x", "c")
NZ = 8
OFFSETS = (0, 4, 1, -3, -1, 3, 2, -2)
WIDTHS = (512, 512)
LAST = (+1, -1)
FIRST = ((0, 1, +1), (0, 1, -1), (1, 1, +1), (1, 1, -1))


def dequantize(codes, scales):
    rows, cols = codes.shape
    blocks = (
        codes.astype(jnp.float32).reshape(rows, cols // BLOCK, BLOCK)
        * jnp.transpose(scales)[:, :, None]
    )
    return blocks.reshape(rows, cols).astype(jnp.bfloat16)


def shift(x, s):
    return lax.ppermute(x, "z", [(i, (i + s) % NZ) for i in range(NZ)])


def order(later, earlier):
    return lax.optimization_barrier((later, earlier))


def swap_rows_features(rows):
    beside, along = [], []
    for slab in range(NZ):
        for place in range(NZ):
            slot = OFFSETS.index((slab - place + 3) % NZ - 3)
            beside.append((slab * NZ + place, slab * NZ + slot))
            along.append((slab * NZ + slot, place * NZ + slot))
    rows = lax.ppermute(rows, ("z", "x", "c"), beside)
    return lax.ppermute(rows, ("z", "x", "c"), along)


def chunk_kernel(places, held, where, rows, *refs):
    heads, refs = refs[: len(places)], refs[len(places) :]
    sums, (away, keep, rows_in, heads_in, sems) = refs[:held], refs[held:]
    copies = []
    for i, ((slot, start), head) in enumerate(zip(places, heads)):
        depth = head.shape[0]
        span = pl.ds(0, depth)
        mine = [pltpu.make_async_copy(head, heads_in.at[i, span], sems.at[i, 2])]
        for side in (0, 1):
            block = rows.at[where[side] * NZ + slot, :, pl.ds(start, depth)]
            mine.append(pltpu.make_async_copy(block, rows_in.at[i, side, :, span], sems.at[i, side]))
        for copy in mine:
            copy.start()
        copies.append(mine)
    totals = [s[...] for s in sums] or [None, None]
    for i, mine in enumerate(copies):
        depth = heads[i].shape[0]
        for copy in mine:
            copy.wait()
        for side in (0, 1):
            part = jnp.dot(
                rows_in[i, side, :, :depth],
                heads_in[i, :depth],
                preferred_element_type=jnp.float32,
            )
            totals[side] = part if totals[side] is None else totals[side] + part
    away[...], keep[...] = totals


def chunk_logits(where, rows, blocks, sums=()):
    places, heads = zip(*blocks)
    tokens, width = rows.shape[1], heads[0].shape[1]
    depth, size = max(h.shape[0] for h in heads), sum(h.size for h in heads)
    out = jax.ShapeDtypeStruct((tokens, width), jnp.float32)
    vmem, loose = pl.BlockSpec(memory_space=pltpu.VMEM), pl.BlockSpec(memory_space=pl.ANY)
    return pl.pallas_call(
        functools.partial(chunk_kernel, places, len(sums)),
        out_shape=(out, out),
        in_specs=[pl.BlockSpec(memory_space=pltpu.SMEM)]
        + [loose] * (1 + len(heads))
        + [vmem] * len(sums),
        out_specs=(vmem, vmem),
        scratch_shapes=[
            pltpu.VMEM((len(heads), 2, tokens, depth), jnp.bfloat16),
            pltpu.VMEM((len(heads), depth, width), jnp.bfloat16),
            pltpu.SemaphoreType.DMA((len(heads), 3)),
        ],
        compiler_params=pltpu.CompilerParams(vmem_limit_bytes=28 * 2**20),
        cost_estimate=pl.CostEstimate(
            flops=4 * tokens * size,
            bytes_accessed=rows.size * 2 + size * 2 + 8 * tokens * width,
            transcendentals=0,
        ),
    )(where, rows, *heads, *sums)


class Ring:
    def __init__(self, own):
        self.block = {(k, 0, way): x for k, x in enumerate(own) for way in (+1, -1)}

    def send(self, k, s):
        for way in (+1, -1):
            if s < 4 or way == LAST[k]:
                self.block[k, s, way] = shift(self.block[k, s - 1, way], way)

    def hold(self, later, keys):
        later, blocks = order(later, [self.block[key] for key in keys])
        self.block.update(zip(keys, blocks))
        return later

    def blocks(self, k, steps):
        found = []
        for s in steps:
            for way in (+1, -1) if s else (+1,):
                if s < 4 or way == LAST[k]:
                    slot = OFFSETS.index(-way * s if s < 4 else 4)
                    found.append(((slot, 0), self.block[k, s, way]))
        return found


def swap_halves(x):
    return lax.ppermute(x, "yh", [(0, 1), (1, 0)])


def body(
    teacher_codes, block_scales, teacher_head, student_hidden, student_head, token_ids, loss_mask
):
    yh = lax.axis_index("yh")
    starts = [sum(WIDTHS[:k]) for k in range(len(WIDTHS))]
    local_rows = dequantize(teacher_codes, block_scales)
    head, local_rows = order(teacher_head, local_rows)
    own = [head[:, a : a + w] for a, w in zip(starts, WIDTHS)]
    own_rows, features = student_hidden.shape
    ring = Ring(own)
    moved = swap_rows_features(local_rows)
    for k in (0, 1):
        ring.send(k, 1)
    moved = ring.hold(moved, FIRST)
    moved = jnp.concatenate([moved, student_hidden], axis=1)
    rows = lax.all_gather(moved, VOCAB, axis=0, tiled=False)
    for s in (2, 3):
        for k in (0, 1):
            ring.send(k, s)

    where = jnp.stack([1 - yh, yh]).astype(jnp.int32)
    where = ring.hold(where, [(0, 3, -1), (0, 3, +1)])
    for k in (0, 1):
        ring.send(k, 4)
    sums = [chunk_logits(where, rows, ring.blocks(k, range(3))) for k in (0, 1)]
    products = [chunk_logits(where, rows, ring.blocks(k, (3, 4)), sums[k]) for k in (0, 1)]
    hidden, products[1] = order(rows, products[1])
    hidden = jnp.transpose(hidden[:, :, teacher_codes.shape[1] :], (1, 0, 2))
    hidden = hidden.reshape(own_rows, 16 * features)
    student_logits = jnp.dot(hidden, student_head, preferred_element_type=jnp.float32)
    parts = [keep + swap_halves(away) for away, keep in products]

    shard_width = student_head.shape[1]
    columns = lax.axis_index(VOCAB) * shard_width + lax.broadcasted_iota(
        jnp.int32, (own_rows, shard_width), 1
    )
    chosen = token_ids[:, None] == columns
    target_part = jnp.sum(jnp.where(chosen, student_logits, 0.0), axis=1)

    teacher_logits = jnp.concatenate(parts, axis=1)

    near_teacher = jnp.max(teacher_logits, axis=1)
    near_student = jnp.max(student_logits, axis=1)
    teacher_exp = jnp.exp(teacher_logits - near_teacher[:, None])
    student_exp = jnp.exp(student_logits - near_student[:, None])
    stats = jnp.stack(
        [
            near_teacher,
            jnp.sum(teacher_exp, axis=1),
            jnp.sum(teacher_exp * (teacher_logits - student_logits), axis=1),
            near_student,
            jnp.sum(student_exp, axis=1),
            target_part,
            jnp.zeros_like(target_part),
            jnp.zeros_like(target_part),
        ]
    )
    stats = lax.all_to_all(
        jnp.broadcast_to(stats[None], (16,) + stats.shape),
        VOCAB,
        split_axis=0,
        concat_axis=0,
        tiled=True,
    )
    top_teacher = jnp.max(stats[:, 0], axis=0)
    top_student = jnp.max(stats[:, 3], axis=0)
    scale_teacher = jnp.exp(stats[:, 0] - top_teacher[None])
    scale_student = jnp.exp(stats[:, 3] - top_student[None])
    sum_teacher = jnp.sum(stats[:, 1] * scale_teacher, axis=0)
    weighted = jnp.sum(stats[:, 2] * scale_teacher, axis=0)
    sum_student = jnp.sum(stats[:, 4] * scale_student, axis=0)
    target = jnp.sum(stats[:, 5], axis=0)

    divergence = (
        weighted / sum_teacher
        - top_teacher
        - jnp.log(sum_teacher)
        + top_student
        + jnp.log(sum_student)
    )
    cross_rows = top_student + jnp.log(sum_student) - target
    live_mask = loss_mask.astype(jnp.float32)
    token_loss = live_mask * (divergence + CROSS_WEIGHT * cross_rows)
    teacher_prob = jnp.exp(teacher_logits - top_teacher[:, None]) / sum_teacher[:, None]
    student_prob = jnp.exp(student_logits - top_student[:, None]) / sum_student[:, None]
    logit_grad = (
        live_mask[:, None]
        * (
            (1.0 + CROSS_WEIGHT) * student_prob
            - teacher_prob
            - CROSS_WEIGHT * chosen.astype(jnp.float32)
        )
    ).astype(jnp.bfloat16)
    hidden_terms = lax.dot_general(
        logit_grad, student_head, (((1,), (1,)), ((), ())), preferred_element_type=jnp.float32
    ).astype(jnp.bfloat16)
    hidden_terms = jnp.transpose(hidden_terms.reshape(own_rows, 16, features), (1, 0, 2))
    hidden_terms = lax.all_to_all(hidden_terms, VOCAB, split_axis=0, concat_axis=0, tiled=True)
    grad_hidden = jnp.sum(hidden_terms.astype(jnp.float32), axis=0).astype(jnp.bfloat16)
    return (grad_hidden, token_loss)


def solution(mesh):
    fine = Mesh(mesh.devices.reshape(2, NZ, 2, 4, 2), GROUP + VOCAB)
    placed = (
        P(VOCAB, GROUP),
        P(GROUP, VOCAB),
        P(GROUP, VOCAB),
        P(GROUP, VOCAB),
        P(None, VOCAB),
        P(GROUP),
        P(GROUP),
    )
    return jax.shard_map(
        body,
        mesh=fine,
        in_specs=placed,
        out_specs=(P(GROUP, VOCAB), P(GROUP)),
        check_vma=False,
    )
```

```python
import functools

import jax
import jax.numpy as jnp
from jax import lax
from jax.experimental import pallas as pl
from jax.experimental.pallas import tpu as pltpu
from jax.sharding import Mesh
from jax.sharding import PartitionSpec as P

BLOCK = 128
CROSS_WEIGHT = 0.5
GROUP = ("yh", "z")
VOCAB = ("yl", "x", "c")
NZ = 8
OFFSETS = (0, 4, 1, -3, -1, 3, 2, -2)
WIDTHS = (512, 512)
LAST = (+1, -1)
FIRST = ((0, 1, +1), (0, 1, -1), (1, 1, +1), (1, 1, -1))


def dequantize(codes, scales):
    rows, cols = codes.shape
    blocks = (
        codes.astype(jnp.float32).reshape(rows, cols // BLOCK, BLOCK)
        * jnp.transpose(scales)[:, :, None]
    )
    return blocks.reshape(rows, cols).astype(jnp.bfloat16)


def shift(x, s):
    return lax.ppermute(x, "z", [(i, (i + s) % NZ) for i in range(NZ)])


def order(later, earlier):
    return lax.optimization_barrier((later, earlier))


def swap_rows_features(rows):
    beside, along = [], []
    for slab in range(NZ):
        for place in range(NZ):
            slot = OFFSETS.index((slab - place + 3) % NZ - 3)
            beside.append((slab * NZ + place, slab * NZ + slot))
            along.append((slab * NZ + slot, place * NZ + slot))
    rows = lax.ppermute(rows, ("z", "x", "c"), beside)
    return lax.ppermute(rows, ("z", "x", "c"), along)


def chunk_kernel(places, chunks, where, rows, *refs):
    steps = len(places)
    heads, refs = refs[: chunks * steps], refs[chunks * steps :]
    (rows_in, heads_in, rows_sems, heads_sems), refs = refs[-4:], refs[:-4]
    sums, outs = refs[: -2 * chunks], refs[-2 * chunks :]
    copies = []
    for i, (slot, start) in enumerate(places):
        depth = heads[i].shape[0]
        mine = []
        for side in (0, 1):
            block = rows.at[where[side] * NZ + slot, :, pl.ds(start, depth)]
            mine.append(pltpu.make_async_copy(block, rows_in.at[i, side], rows_sems.at[i, side]))
        for k in range(chunks):
            j = k * steps + i
            mine.append(pltpu.make_async_copy(heads[j], heads_in.at[j], heads_sems.at[j]))
        for copy in mine:
            copy.start()
        copies.append(mine)
    totals = [s[...] for s in sums] or [None] * (2 * chunks)
    for i, mine in enumerate(copies):
        for copy in mine:
            copy.wait()
        for k in range(chunks):
            for side in (0, 1):
                part = jnp.dot(
                    rows_in[i, side],
                    heads_in[k * steps + i],
                    preferred_element_type=jnp.float32,
                )
                total = totals[2 * k + side]
                totals[2 * k + side] = part if total is None else total + part
    for out, total in zip(outs, totals):
        out[...] = total


def chunk_logits(where, rows, chunks, sums=()):
    places = [place for place, _ in chunks[0]]
    heads = [head for blocks in chunks for _, head in blocks]
    tokens, (depth, width) = rows.shape[1], heads[0].shape
    size = sum(h.size for h in heads)
    out = jax.ShapeDtypeStruct((tokens, width), jnp.float32)
    vmem, loose = pl.BlockSpec(memory_space=pltpu.VMEM), pl.BlockSpec(memory_space=pl.ANY)
    return pl.pallas_call(
        functools.partial(chunk_kernel, places, len(chunks)),
        out_shape=(out,) * (2 * len(chunks)),
        in_specs=[pl.BlockSpec(memory_space=pltpu.SMEM)]
        + [loose] * (1 + len(heads))
        + [vmem] * len(sums),
        out_specs=(vmem,) * (2 * len(chunks)),
        scratch_shapes=[
            pltpu.VMEM((len(places), 2, tokens, depth), jnp.bfloat16),
            pltpu.VMEM((len(heads), depth, width), jnp.bfloat16),
            pltpu.SemaphoreType.DMA((len(places), 2)),
            pltpu.SemaphoreType.DMA((len(heads),)),
        ],
        compiler_params=pltpu.CompilerParams(vmem_limit_bytes=50 * 2**20),
        cost_estimate=pl.CostEstimate(
            flops=4 * tokens * size,
            bytes_accessed=rows.size * 2 + size * 2 + 8 * tokens * width,
            transcendentals=0,
        ),
    )(where, rows, *heads, *sums)


class Ring:
    def __init__(self, own):
        self.block = {(k, 0, way): x for k, x in enumerate(own) for way in (+1, -1)}

    def send(self, k, s):
        for way in (+1, -1):
            if s < 4 or way == LAST[k]:
                self.block[k, s, way] = shift(self.block[k, s - 1, way], way)

    def hold(self, later, keys):
        later, blocks = order(later, [self.block[key] for key in keys])
        self.block.update(zip(keys, blocks))
        return later

    def blocks(self, k, steps):
        found = []
        for s in steps:
            for way in (+1, -1) if s else (+1,):
                if s < 4 or way == LAST[k]:
                    slot = OFFSETS.index(-way * s if s < 4 else 4)
                    found.append(((slot, 0), self.block[k, s, way]))
        return found


def gradient_kernel(first, per_row, ids, teacher, student, head, out, grad):
    @pl.when(pl.program_id(0) == 0)
    def _():
        rows = per_row[...]
        teacher_part = rows[:, 1:2] * jnp.exp(teacher[...] - rows[:, 0:1])
        student_part = rows[:, 3:4] * jnp.exp(student[...] - rows[:, 2:3])
        columns = lax.broadcasted_iota(jnp.int32, teacher.shape, 1) + first[0]
        chosen = jnp.where(ids[...] == columns, rows[:, 4:5], 0.0)
        grad[...] = (student_part - teacher_part - chosen).astype(grad.dtype)

    terms = lax.dot_general(
        grad[...], head[...], (((1,), (1,)), ((), ())), preferred_element_type=jnp.float32
    )
    width = out.shape[2]
    for k in range(out.shape[0]):
        out[k] = terms[:, k * width : (k + 1) * width].astype(out.dtype)


def gradient_terms(first, per_row, ids, teacher, student, head, width):
    tokens, shard = teacher.shape
    features, step = head.shape[0], 4
    smem = pl.BlockSpec(memory_space=pltpu.SMEM)
    whole = pl.BlockSpec((tokens, shard), lambda i: (0, 0))
    return pl.pallas_call(
        gradient_kernel,
        grid=(features // (step * width),),
        out_shape=jax.ShapeDtypeStruct((features // width, tokens, width), jnp.bfloat16),
        in_specs=[
            smem,
            pl.BlockSpec(per_row.shape, lambda i: (0, 0)),
            pl.BlockSpec(ids.shape, lambda i: (0, 0)),
            whole,
            whole,
            pl.BlockSpec((step * width, shard), lambda i: (i, 0)),
        ],
        out_specs=pl.BlockSpec((step, tokens, width), lambda i: (i, 0, 0)),
        scratch_shapes=[pltpu.VMEM((tokens, shard), jnp.bfloat16)],
        compiler_params=pltpu.CompilerParams(vmem_limit_bytes=24 * 2**20),
        cost_estimate=pl.CostEstimate(
            flops=2 * tokens * shard * features,
            bytes_accessed=head.size * 2 + 8 * tokens * shard + 2 * tokens * features,
            transcendentals=2 * tokens * shard,
        ),
    )(first, per_row, ids, teacher, student, head)


def swap_halves(x):
    return lax.ppermute(x, "yh", [(0, 1), (1, 0)])


def body(
    teacher_codes, block_scales, teacher_head, student_hidden, student_head, token_ids, loss_mask
):
    yh = lax.axis_index("yh")
    starts = [sum(WIDTHS[:k]) for k in range(len(WIDTHS))]
    local_rows = dequantize(teacher_codes, block_scales)
    head, local_rows = order(teacher_head, local_rows)
    own = [head[:, a : a + w] for a, w in zip(starts, WIDTHS)]
    own_rows, features = student_hidden.shape
    ring = Ring(own)
    moved = swap_rows_features(local_rows)
    for k in (0, 1):
        ring.send(k, 1)
    moved = ring.hold(moved, FIRST)
    moved = jnp.concatenate([moved, student_hidden], axis=1)
    rows = lax.all_gather(moved, VOCAB, axis=0, tiled=False)
    for s in (2, 3):
        for k in (0, 1):
            ring.send(k, s)

    where = jnp.stack([1 - yh, yh]).astype(jnp.int32)
    for k in (0, 1):
        ring.send(k, 4)
    sums = chunk_logits(where, rows, [ring.blocks(k, range(3)) for k in (0, 1)])
    products = [
        chunk_logits(where, rows, [ring.blocks(k, (3, 4))], sums[2 * k : 2 * k + 2]) for k in (0, 1)
    ]
    hidden, products[1] = order(rows, products[1])
    hidden = jnp.transpose(hidden[:, :, teacher_codes.shape[1] :], (1, 0, 2))
    hidden = hidden.reshape(own_rows, 16 * features)
    student_logits = jnp.dot(hidden, student_head, preferred_element_type=jnp.float32)
    parts = [keep + swap_halves(away) for away, keep in products]

    shard_width = student_head.shape[1]
    columns = lax.axis_index(VOCAB) * shard_width + lax.broadcasted_iota(
        jnp.int32, (own_rows, shard_width), 1
    )
    chosen = token_ids[:, None] == columns
    target_part = jnp.sum(jnp.where(chosen, student_logits, 0.0), axis=1)

    teacher_logits = jnp.concatenate(parts, axis=1)

    near_teacher = jnp.max(teacher_logits, axis=1)
    near_student = jnp.max(student_logits, axis=1)
    teacher_exp = jnp.exp(teacher_logits - near_teacher[:, None])
    student_exp = jnp.exp(student_logits - near_student[:, None])
    stats = jnp.stack(
        [
            near_teacher,
            jnp.sum(teacher_exp, axis=1),
            jnp.sum(teacher_exp * (teacher_logits - student_logits), axis=1),
            near_student,
            jnp.sum(student_exp, axis=1),
            target_part,
            jnp.zeros_like(target_part),
            jnp.zeros_like(target_part),
        ]
    )
    stats = lax.all_to_all(
        jnp.broadcast_to(stats[None], (16,) + stats.shape),
        VOCAB,
        split_axis=0,
        concat_axis=0,
        tiled=True,
    )
    top_teacher = jnp.max(stats[:, 0], axis=0)
    top_student = jnp.max(stats[:, 3], axis=0)
    scale_teacher = jnp.exp(stats[:, 0] - top_teacher[None])
    scale_student = jnp.exp(stats[:, 3] - top_student[None])
    sum_teacher = jnp.sum(stats[:, 1] * scale_teacher, axis=0)
    weighted = jnp.sum(stats[:, 2] * scale_teacher, axis=0)
    sum_student = jnp.sum(stats[:, 4] * scale_student, axis=0)
    target = jnp.sum(stats[:, 5], axis=0)

    divergence = (
        weighted / sum_teacher
        - top_teacher
        - jnp.log(sum_teacher)
        + top_student
        + jnp.log(sum_student)
    )
    cross_rows = top_student + jnp.log(sum_student) - target
    live_mask = loss_mask.astype(jnp.float32)
    token_loss = live_mask * (divergence + CROSS_WEIGHT * cross_rows)
    zero = jnp.zeros_like(live_mask)
    per_row = jnp.stack(
        [
            top_teacher,
            live_mask / sum_teacher,
            top_student,
            (1.0 + CROSS_WEIGHT) * live_mask / sum_student,
            CROSS_WEIGHT * live_mask,
            zero,
            zero,
            zero,
        ]
    )
    hidden_terms = gradient_terms(
        (lax.axis_index(VOCAB) * shard_width).astype(jnp.int32)[None],
        jnp.transpose(per_row),
        token_ids[:, None],
        teacher_logits,
        student_logits,
        student_head,
        features,
    )
    hidden_terms = lax.all_to_all(hidden_terms, VOCAB, split_axis=0, concat_axis=0, tiled=True)
    grad_hidden = jnp.sum(hidden_terms.astype(jnp.float32), axis=0).astype(jnp.bfloat16)
    return (grad_hidden, token_loss)


def solution(mesh):
    fine = Mesh(mesh.devices.reshape(2, NZ, 2, 4, 2), GROUP + VOCAB)
    placed = (
        P(VOCAB, GROUP),
        P(GROUP, VOCAB),
        P(GROUP, VOCAB),
        P(GROUP, VOCAB),
        P(None, VOCAB),
        P(GROUP),
        P(GROUP),
    )
    return jax.shard_map(
        body,
        mesh=fine,
        in_specs=placed,
        out_specs=(P(GROUP, VOCAB), P(GROUP)),
        check_vma=False,
    )
```

```python
import functools

import jax
import jax.numpy as jnp
from jax import lax
from jax.experimental import pallas as pl
from jax.experimental.pallas import tpu as pltpu
from jax.sharding import Mesh
from jax.sharding import PartitionSpec as P

BLOCK = 128
CROSS_WEIGHT = 0.5
GROUP = ("yh", "z")
VOCAB = ("yl", "x", "c")
NZ = 8
OFFSETS = (0, 4, 1, -3, -1, 3, 2, -2)
WIDTHS = (512, 512)
LAST = (+1, -1)


def dequantize(codes, scales):
    rows, cols = codes.shape
    blocks = (
        codes.astype(jnp.float32).reshape(rows, cols // BLOCK, BLOCK)
        * jnp.transpose(scales)[:, :, None]
    )
    return blocks.reshape(rows, cols).astype(jnp.bfloat16)


def shift(x, s):
    return lax.ppermute(x, "z", [(i, (i + s) % NZ) for i in range(NZ)])


def order(later, earlier):
    return lax.optimization_barrier((later, earlier))


def swap_rows_features(rows):
    beside, along = [], []
    for slab in range(NZ):
        for place in range(NZ):
            slot = OFFSETS.index((slab - place + 3) % NZ - 3)
            beside.append((slab * NZ + place, slab * NZ + slot))
            along.append((slab * NZ + slot, place * NZ + slot))
    rows = lax.ppermute(rows, ("z", "x", "c"), beside)
    return lax.ppermute(rows, ("z", "x", "c"), along)


def chunk_kernel(places, chunks, where, rows, *refs):
    steps = len(places)
    heads, refs = refs[: chunks * steps], refs[chunks * steps :]
    (rows_in, heads_in, rows_sems, heads_sems), refs = refs[-4:], refs[:-4]
    sums, outs = refs[: -2 * chunks], refs[-2 * chunks :]
    copies = []
    for i, (slot, start) in enumerate(places):
        depth = heads[i].shape[0]
        mine = []
        for side in (0, 1):
            block = rows.at[where[side] * NZ + slot, :, pl.ds(start, depth)]
            mine.append(pltpu.make_async_copy(block, rows_in.at[i, side], rows_sems.at[i, side]))
        for k in range(chunks):
            j = k * steps + i
            mine.append(pltpu.make_async_copy(heads[j], heads_in.at[j], heads_sems.at[j]))
        for copy in mine:
            copy.start()
        copies.append(mine)
    totals = [s[...] for s in sums] or [None] * (2 * chunks)
    for i, mine in enumerate(copies):
        for copy in mine:
            copy.wait()
        for k in range(chunks):
            for side in (0, 1):
                part = jnp.dot(
                    rows_in[i, side],
                    heads_in[k * steps + i],
                    preferred_element_type=jnp.float32,
                )
                total = totals[2 * k + side]
                totals[2 * k + side] = part if total is None else total + part
    for out, total in zip(outs, totals):
        out[...] = total


def chunk_logits(where, rows, chunks, sums=()):
    places = [place for place, _ in chunks[0]]
    heads = [head for blocks in chunks for _, head in blocks]
    tokens, (depth, width) = rows.shape[1], heads[0].shape
    size = sum(h.size for h in heads)
    out = jax.ShapeDtypeStruct((tokens, width), jnp.float32)
    vmem, loose = pl.BlockSpec(memory_space=pltpu.VMEM), pl.BlockSpec(memory_space=pl.ANY)
    return pl.pallas_call(
        functools.partial(chunk_kernel, places, len(chunks)),
        out_shape=(out,) * (2 * len(chunks)),
        in_specs=[pl.BlockSpec(memory_space=pltpu.SMEM)]
        + [loose] * (1 + len(heads))
        + [vmem] * len(sums),
        out_specs=(vmem,) * (2 * len(chunks)),
        scratch_shapes=[
            pltpu.VMEM((len(places), 2, tokens, depth), jnp.bfloat16),
            pltpu.VMEM((len(heads), depth, width), jnp.bfloat16),
            pltpu.SemaphoreType.DMA((len(places), 2)),
            pltpu.SemaphoreType.DMA((len(heads),)),
        ],
        compiler_params=pltpu.CompilerParams(vmem_limit_bytes=50 * 2**20),
        cost_estimate=pl.CostEstimate(
            flops=4 * tokens * size,
            bytes_accessed=rows.size * 2 + size * 2 + 8 * tokens * width,
            transcendentals=0,
        ),
    )(where, rows, *heads, *sums)


class Ring:
    def __init__(self, own, first):
        self.block = {}
        for k, width in enumerate(WIDTHS):
            columns = slice(sum(WIDTHS[:k]), sum(WIDTHS[:k]) + width)
            for way, arrived in zip((+1, -1), first):
                self.block[k, 0, way] = own[:, columns]
                self.block[k, 1, way] = arrived[:, columns]

    def send(self, k, s):
        for way in (+1, -1):
            if s < 4 or way == LAST[k]:
                self.block[k, s, way] = shift(self.block[k, s - 1, way], way)

    def hold(self, later, keys):
        later, blocks = order(later, [self.block[key] for key in keys])
        self.block.update(zip(keys, blocks))
        return later

    def blocks(self, k, steps):
        found = []
        for s in steps:
            for way in (+1, -1) if s else (+1,):
                if s < 4 or way == LAST[k]:
                    slot = OFFSETS.index(-way * s if s < 4 else 4)
                    found.append(((slot, 0), self.block[k, s, way]))
        return found


def gradient_kernel(first, per_row, ids, teacher, student, head, out, grad):
    @pl.when(pl.program_id(0) == 0)
    def _():
        rows = per_row[...]
        teacher_part = rows[:, 1:2] * jnp.exp(teacher[...] - rows[:, 0:1])
        student_part = rows[:, 3:4] * jnp.exp(student[...] - rows[:, 2:3])
        columns = lax.broadcasted_iota(jnp.int32, teacher.shape, 1) + first[0]
        chosen = jnp.where(ids[...] == columns, rows[:, 4:5], 0.0)
        grad[...] = (student_part - teacher_part - chosen).astype(grad.dtype)

    terms = lax.dot_general(
        grad[...], head[...], (((1,), (1,)), ((), ())), preferred_element_type=jnp.float32
    )
    width = out.shape[2]
    for k in range(out.shape[0]):
        out[k] = terms[:, k * width : (k + 1) * width].astype(out.dtype)


def gradient_terms(first, per_row, ids, teacher, student, head, width):
    tokens, shard = teacher.shape
    features, step = head.shape[0], 4
    smem = pl.BlockSpec(memory_space=pltpu.SMEM)
    whole = pl.BlockSpec((tokens, shard), lambda i: (0, 0))
    return pl.pallas_call(
        gradient_kernel,
        grid=(features // (step * width),),
        out_shape=jax.ShapeDtypeStruct((features // width, tokens, width), jnp.bfloat16),
        in_specs=[
            smem,
            pl.BlockSpec(per_row.shape, lambda i: (0, 0)),
            pl.BlockSpec(ids.shape, lambda i: (0, 0)),
            whole,
            whole,
            pl.BlockSpec((step * width, shard), lambda i: (i, 0)),
        ],
        out_specs=pl.BlockSpec((step, tokens, width), lambda i: (i, 0, 0)),
        scratch_shapes=[pltpu.VMEM((tokens, shard), jnp.bfloat16)],
        compiler_params=pltpu.CompilerParams(vmem_limit_bytes=24 * 2**20),
        cost_estimate=pl.CostEstimate(
            flops=2 * tokens * shard * features,
            bytes_accessed=head.size * 2 + 8 * tokens * shard + 2 * tokens * features,
            transcendentals=2 * tokens * shard,
        ),
    )(first, per_row, ids, teacher, student, head)


def swap_halves(x):
    return lax.ppermute(x, "yh", [(0, 1), (1, 0)])


def body(
    teacher_codes, block_scales, teacher_head, student_hidden, student_head, token_ids, loss_mask
):
    yh = lax.axis_index("yh")
    local_rows = dequantize(teacher_codes, block_scales)
    own_rows, features = student_hidden.shape
    first = [shift(teacher_head, way) for way in (+1, -1)]
    moved = swap_rows_features(local_rows)
    moved, first = order(moved, first)
    ring = Ring(teacher_head, first)
    moved = jnp.concatenate([moved, student_hidden], axis=1)
    rows = lax.all_gather(moved, VOCAB, axis=0, tiled=False)
    for s in (2, 3):
        for k in (0, 1):
            ring.send(k, s)

    where = jnp.stack([1 - yh, yh]).astype(jnp.int32)
    for k in (0, 1):
        ring.send(k, 4)
    sums = chunk_logits(where, rows, [ring.blocks(k, range(3)) for k in (0, 1)])
    products = [
        chunk_logits(where, rows, [ring.blocks(k, (3, 4))], sums[2 * k : 2 * k + 2]) for k in (0, 1)
    ]
    hidden, products[1] = order(rows, products[1])
    hidden = jnp.transpose(hidden[:, :, teacher_codes.shape[1] :], (1, 0, 2))
    hidden = hidden.reshape(own_rows, 16 * features)
    student_logits = jnp.dot(hidden, student_head, preferred_element_type=jnp.float32)
    parts = [keep + swap_halves(away) for away, keep in products]

    shard_width = student_head.shape[1]
    columns = lax.axis_index(VOCAB) * shard_width + lax.broadcasted_iota(
        jnp.int32, (own_rows, shard_width), 1
    )
    chosen = token_ids[:, None] == columns
    target_part = jnp.sum(jnp.where(chosen, student_logits, 0.0), axis=1)

    teacher_logits = jnp.concatenate(parts, axis=1)

    near_teacher = jnp.max(teacher_logits, axis=1)
    near_student = jnp.max(student_logits, axis=1)
    teacher_exp = jnp.exp(teacher_logits - near_teacher[:, None])
    student_exp = jnp.exp(student_logits - near_student[:, None])
    stats = jnp.stack(
        [
            near_teacher,
            jnp.sum(teacher_exp, axis=1),
            jnp.sum(teacher_exp * (teacher_logits - student_logits), axis=1),
            near_student,
            jnp.sum(student_exp, axis=1),
            target_part,
            jnp.zeros_like(target_part),
            jnp.zeros_like(target_part),
        ]
    )
    stats = lax.all_to_all(
        jnp.broadcast_to(stats[None], (16,) + stats.shape),
        VOCAB,
        split_axis=0,
        concat_axis=0,
        tiled=True,
    )
    top_teacher = jnp.max(stats[:, 0], axis=0)
    top_student = jnp.max(stats[:, 3], axis=0)
    scale_teacher = jnp.exp(stats[:, 0] - top_teacher[None])
    scale_student = jnp.exp(stats[:, 3] - top_student[None])
    sum_teacher = jnp.sum(stats[:, 1] * scale_teacher, axis=0)
    weighted = jnp.sum(stats[:, 2] * scale_teacher, axis=0)
    sum_student = jnp.sum(stats[:, 4] * scale_student, axis=0)
    target = jnp.sum(stats[:, 5], axis=0)

    divergence = (
        weighted / sum_teacher
        - top_teacher
        - jnp.log(sum_teacher)
        + top_student
        + jnp.log(sum_student)
    )
    cross_rows = top_student + jnp.log(sum_student) - target
    live_mask = loss_mask.astype(jnp.float32)
    token_loss = live_mask * (divergence + CROSS_WEIGHT * cross_rows)
    zero = jnp.zeros_like(live_mask)
    per_row = jnp.stack(
        [
            top_teacher,
            live_mask / sum_teacher,
            top_student,
            (1.0 + CROSS_WEIGHT) * live_mask / sum_student,
            CROSS_WEIGHT * live_mask,
            zero,
            zero,
            zero,
        ]
    )
    hidden_terms = gradient_terms(
        (lax.axis_index(VOCAB) * shard_width).astype(jnp.int32)[None],
        jnp.transpose(per_row),
        token_ids[:, None],
        teacher_logits,
        student_logits,
        student_head,
        features,
    )
    hidden_terms = lax.all_to_all(hidden_terms, VOCAB, split_axis=0, concat_axis=0, tiled=True)
    grad_hidden = jnp.sum(hidden_terms.astype(jnp.float32), axis=0).astype(jnp.bfloat16)
    return (grad_hidden, token_loss)


def solution(mesh):
    fine = Mesh(mesh.devices.reshape(2, NZ, 2, 4, 2), GROUP + VOCAB)
    placed = (
        P(VOCAB, GROUP),
        P(GROUP, VOCAB),
        P(GROUP, VOCAB),
        P(GROUP, VOCAB),
        P(None, VOCAB),
        P(GROUP),
        P(GROUP),
    )
    return jax.shard_map(
        body,
        mesh=fine,
        in_specs=placed,
        out_specs=(P(GROUP, VOCAB), P(GROUP)),
        check_vma=False,
    )
```

```python
import functools

import jax
import jax.numpy as jnp
from jax import lax
from jax.experimental import pallas as pl
from jax.experimental.pallas import tpu as pltpu
from jax.sharding import Mesh
from jax.sharding import PartitionSpec as P

BLOCK = 128
CROSS_WEIGHT = 0.5
GROUP = ("yh", "z")
VOCAB = ("yl", "x", "c")
NZ = 8
OFFSETS = (0, 4, 1, -3, -1, 3, 2, -2)
WIDTHS = (512, 512)
LAST = (+1, -1)


def dequantize(codes, scales):
    rows, cols = codes.shape
    blocks = (
        codes.astype(jnp.float32).reshape(rows, cols // BLOCK, BLOCK)
        * jnp.transpose(scales)[:, :, None]
    )
    return blocks.reshape(rows, cols).astype(jnp.bfloat16)


def shift(x, s):
    return lax.ppermute(x, "z", [(i, (i + s) % NZ) for i in range(NZ)])


def order(later, earlier):
    return lax.optimization_barrier((later, earlier))


def swap_rows_features(rows):
    beside, along = [], []
    for slab in range(NZ):
        for place in range(NZ):
            slot = OFFSETS.index((slab - place + 3) % NZ - 3)
            beside.append((slab * NZ + place, slab * NZ + slot))
            along.append((slab * NZ + slot, place * NZ + slot))
    rows = lax.ppermute(rows, ("z", "x", "c"), beside)
    return lax.ppermute(rows, ("z", "x", "c"), along)


def chunk_kernel(places, chunks, where, rows, *refs):
    steps = len(places)
    heads, refs = refs[: chunks * steps], refs[chunks * steps :]
    (rows_in, heads_in, rows_sems, heads_sems), refs = refs[-4:], refs[:-4]
    sums, outs = refs[: -2 * chunks], refs[-2 * chunks :]
    copies = []
    for i, (slot, start) in enumerate(places):
        depth = heads[i].shape[0]
        mine = []
        for side in (0, 1):
            block = rows.at[where[side] * NZ + slot, :, pl.ds(start, depth)]
            mine.append(pltpu.make_async_copy(block, rows_in.at[i, side], rows_sems.at[i, side]))
        for k in range(chunks):
            j = k * steps + i
            mine.append(pltpu.make_async_copy(heads[j], heads_in.at[j], heads_sems.at[j]))
        for copy in mine:
            copy.start()
        copies.append(mine)
    totals = [s[...] for s in sums] or [None] * (2 * chunks)
    for i, mine in enumerate(copies):
        for copy in mine:
            copy.wait()
        for k in range(chunks):
            for side in (0, 1):
                part = jnp.dot(
                    rows_in[i, side],
                    heads_in[k * steps + i],
                    preferred_element_type=jnp.float32,
                )
                total = totals[2 * k + side]
                totals[2 * k + side] = part if total is None else total + part
    for out, total in zip(outs, totals):
        out[...] = total


def chunk_logits(where, rows, chunks, sums=()):
    places = [place for place, _ in chunks[0]]
    heads = [head for blocks in chunks for _, head in blocks]
    tokens, (depth, width) = rows.shape[1], heads[0].shape
    size = sum(h.size for h in heads)
    out = jax.ShapeDtypeStruct((tokens, width), jnp.float32)
    vmem, loose = pl.BlockSpec(memory_space=pltpu.VMEM), pl.BlockSpec(memory_space=pl.ANY)
    return pl.pallas_call(
        functools.partial(chunk_kernel, places, len(chunks)),
        out_shape=(out,) * (2 * len(chunks)),
        in_specs=[pl.BlockSpec(memory_space=pltpu.SMEM)]
        + [loose] * (1 + len(heads))
        + [vmem] * len(sums),
        out_specs=(vmem,) * (2 * len(chunks)),
        scratch_shapes=[
            pltpu.VMEM((len(places), 2, tokens, depth), jnp.bfloat16),
            pltpu.VMEM((len(heads), depth, width), jnp.bfloat16),
            pltpu.SemaphoreType.DMA((len(places), 2)),
            pltpu.SemaphoreType.DMA((len(heads),)),
        ],
        compiler_params=pltpu.CompilerParams(vmem_limit_bytes=50 * 2**20),
        cost_estimate=pl.CostEstimate(
            flops=4 * tokens * size,
            bytes_accessed=rows.size * 2 + size * 2 + 8 * tokens * width,
            transcendentals=0,
        ),
    )(where, rows, *heads, *sums)


class Ring:
    def __init__(self, own, first):
        self.block = {}
        for k, width in enumerate(WIDTHS):
            columns = slice(sum(WIDTHS[:k]), sum(WIDTHS[:k]) + width)
            for way, arrived in zip((+1, -1), first):
                self.block[k, 0, way] = own[:, columns]
                self.block[k, 1, way] = arrived[:, columns]

    def send(self, k, s):
        for way in (+1, -1):
            if s < 4 or way == LAST[k]:
                self.block[k, s, way] = shift(self.block[k, s - 1, way], way)

    def hold(self, later, keys):
        later, blocks = order(later, [self.block[key] for key in keys])
        self.block.update(zip(keys, blocks))
        return later

    def blocks(self, k, steps):
        found = []
        for s in steps:
            for way in (+1, -1) if s else (+1,):
                if s < 4 or way == LAST[k]:
                    slot = OFFSETS.index(-way * s if s < 4 else 4)
                    found.append(((slot, 0), self.block[k, s, way]))
        return found


def gradient_kernel(first, per_row, ids, teacher, student, head, mine, other, grad):
    @pl.when(pl.program_id(0) == 0)
    def _():
        rows = per_row[...]
        teacher_part = rows[:, 1:2] * jnp.exp(teacher[...] - rows[:, 0:1])
        student_part = rows[:, 3:4] * jnp.exp(student[...] - rows[:, 2:3])
        columns = lax.broadcasted_iota(jnp.int32, teacher.shape, 1) + first[0]
        chosen = jnp.where(ids[...] == columns, rows[:, 4:5], 0.0)
        grad[...] = (student_part - teacher_part - chosen).astype(grad.dtype)

    terms = lax.dot_general(
        grad[...], head[...], (((1,), (1,)), ((), ())), preferred_element_type=jnp.float32
    )
    width = mine.shape[2]
    for k in range(mine.shape[0]):
        even = terms[:, 2 * k * width : (2 * k + 1) * width]
        odd = terms[:, (2 * k + 1) * width : (2 * k + 2) * width]
        mine[k] = jnp.where(first[1] == 0, even, odd)
        other[k] = jnp.where(first[1] == 0, odd, even)


def gradient_terms(first, per_row, ids, teacher, student, head, width):
    tokens, shard = teacher.shape
    features, step = head.shape[0], 4
    smem = pl.BlockSpec(memory_space=pltpu.SMEM)
    whole = pl.BlockSpec((tokens, shard), lambda i: (0, 0))
    return pl.pallas_call(
        gradient_kernel,
        grid=(features // (step * width),),
        out_shape=(jax.ShapeDtypeStruct((features // width // 2, tokens, width), jnp.float32),) * 2,
        in_specs=[
            smem,
            pl.BlockSpec(per_row.shape, lambda i: (0, 0)),
            pl.BlockSpec(ids.shape, lambda i: (0, 0)),
            whole,
            whole,
            pl.BlockSpec((step * width, shard), lambda i: (i, 0)),
        ],
        out_specs=(pl.BlockSpec((step // 2, tokens, width), lambda i: (i, 0, 0)),) * 2,
        scratch_shapes=[pltpu.VMEM((tokens, shard), jnp.bfloat16)],
        compiler_params=pltpu.CompilerParams(vmem_limit_bytes=24 * 2**20),
        cost_estimate=pl.CostEstimate(
            flops=2 * tokens * shard * features,
            bytes_accessed=head.size * 2 + 8 * tokens * shard + 2 * tokens * features,
            transcendentals=2 * tokens * shard,
        ),
    )(first, per_row, ids, teacher, student, head)


def swap_halves(x):
    return lax.ppermute(x, "yh", [(0, 1), (1, 0)])


def body(
    teacher_codes, block_scales, teacher_head, student_hidden, student_head, token_ids, loss_mask
):
    yh = lax.axis_index("yh")
    local_rows = dequantize(teacher_codes, block_scales)
    own_rows, features = student_hidden.shape
    first = [shift(teacher_head, way) for way in (+1, -1)]
    moved = swap_rows_features(local_rows)
    moved, first = order(moved, first)
    ring = Ring(teacher_head, first)
    moved = jnp.concatenate([moved, student_hidden], axis=1)
    rows = lax.all_gather(moved, VOCAB, axis=0, tiled=False)
    for s in (2, 3):
        for k in (0, 1):
            ring.send(k, s)

    where = jnp.stack([1 - yh, yh]).astype(jnp.int32)
    for k in (0, 1):
        ring.send(k, 4)
    sums = chunk_logits(where, rows, [ring.blocks(k, range(3)) for k in (0, 1)])
    products = [
        chunk_logits(where, rows, [ring.blocks(k, (3, 4))], sums[2 * k : 2 * k + 2]) for k in (0, 1)
    ]
    hidden, products[1] = order(rows, products[1])
    hidden = jnp.transpose(hidden[:, :, teacher_codes.shape[1] :], (1, 0, 2))
    hidden = hidden.reshape(own_rows, 16 * features)
    student_logits = jnp.dot(hidden, student_head, preferred_element_type=jnp.float32)
    parts = [keep + swap_halves(away) for away, keep in products]

    shard_width = student_head.shape[1]
    columns = lax.axis_index(VOCAB) * shard_width + lax.broadcasted_iota(
        jnp.int32, (own_rows, shard_width), 1
    )
    chosen = token_ids[:, None] == columns
    target_part = jnp.sum(jnp.where(chosen, student_logits, 0.0), axis=1)

    teacher_logits = jnp.concatenate(parts, axis=1)

    near_teacher = jnp.max(teacher_logits, axis=1)
    near_student = jnp.max(student_logits, axis=1)
    teacher_exp = jnp.exp(teacher_logits - near_teacher[:, None])
    student_exp = jnp.exp(student_logits - near_student[:, None])
    stats = jnp.stack(
        [
            near_teacher,
            jnp.sum(teacher_exp, axis=1),
            jnp.sum(teacher_exp * (teacher_logits - student_logits), axis=1),
            near_student,
            jnp.sum(student_exp, axis=1),
            target_part,
            jnp.zeros_like(target_part),
            jnp.zeros_like(target_part),
        ]
    )
    stats = lax.all_to_all(
        jnp.broadcast_to(stats[None], (16,) + stats.shape),
        VOCAB,
        split_axis=0,
        concat_axis=0,
        tiled=True,
    )
    top_teacher = jnp.max(stats[:, 0], axis=0)
    top_student = jnp.max(stats[:, 3], axis=0)
    scale_teacher = jnp.exp(stats[:, 0] - top_teacher[None])
    scale_student = jnp.exp(stats[:, 3] - top_student[None])
    sum_teacher = jnp.sum(stats[:, 1] * scale_teacher, axis=0)
    weighted = jnp.sum(stats[:, 2] * scale_teacher, axis=0)
    sum_student = jnp.sum(stats[:, 4] * scale_student, axis=0)
    target = jnp.sum(stats[:, 5], axis=0)

    divergence = (
        weighted / sum_teacher
        - top_teacher
        - jnp.log(sum_teacher)
        + top_student
        + jnp.log(sum_student)
    )
    cross_rows = top_student + jnp.log(sum_student) - target
    live_mask = loss_mask.astype(jnp.float32)
    token_loss = live_mask * (divergence + CROSS_WEIGHT * cross_rows)
    zero = jnp.zeros_like(live_mask)
    per_row = jnp.stack(
        [
            top_teacher,
            live_mask / sum_teacher,
            top_student,
            (1.0 + CROSS_WEIGHT) * live_mask / sum_student,
            CROSS_WEIGHT * live_mask,
            zero,
            zero,
            zero,
        ]
    )
    mine, other = gradient_terms(
        jnp.stack([lax.axis_index(VOCAB) * shard_width, lax.axis_index("c")]).astype(jnp.int32),
        jnp.transpose(per_row),
        token_ids[:, None],
        teacher_logits,
        student_logits,
        student_head,
        features,
    )
    mine = mine + lax.ppermute(other, "c", [(0, 1), (1, 0)])
    hidden_terms = lax.all_to_all(
        mine.astype(jnp.bfloat16), ("yl", "x"), split_axis=0, concat_axis=0, tiled=True
    )
    grad_hidden = jnp.sum(hidden_terms.astype(jnp.float32), axis=0).astype(jnp.bfloat16)
    return (grad_hidden, token_loss)


def solution(mesh):
    fine = Mesh(mesh.devices.reshape(2, NZ, 2, 4, 2), GROUP + VOCAB)
    placed = (
        P(VOCAB, GROUP),
        P(GROUP, VOCAB),
        P(GROUP, VOCAB),
        P(GROUP, VOCAB),
        P(None, VOCAB),
        P(GROUP),
        P(GROUP),
    )
    return jax.shard_map(
        body,
        mesh=fine,
        in_specs=placed,
        out_specs=(P(GROUP, VOCAB), P(GROUP)),
        check_vma=False,
    )
```
